32 devices in a mesh: section: 2 (over y), dp: 2 (over x), tensor: 8 (over z, core).
Axes of the slice: x: 2, y: 2, z: 4, core: 2. Of those that a mesh axis runs over, the one named last changes fastest.
Arguments:
- incoming: bfloat16 [2, 512, 12288], P('section', 'tensor', 'dp'), may hold values from -24 to 24, as said below
- norm_gain: float32 [2, 12288], P('section', 'dp'), may hold values from 0.1 to 1.9
- norm_shift: float32 [2, 12288], P('section', 'dp'), may hold values from -3 to 3
- up_weight: bfloat16 [2, 12288, 24576], P('section', 'dp', 'tensor'), may hold values from -0.0546875 to 0.0546875
- up_bias: float32 [2, 24576], P('section', 'tensor'), may hold values from -4 to 4
- down_weight: bfloat16 [2, 24576, 12288], P('section', 'tensor', 'dp'), may hold values from -0.0390625 to 0.0390625
- down_bias: float32 [2, 12288], P('section', 'dp'), may hold values from -3 to 3
Outputs:
- rotated: bfloat16 [2, 512, 12288], P('section', 'tensor', 'dp')
The draws below stay inside these ranges and needn't reach their ends.
Inputs may be any that keep to these rules, and one draw needn't show every extreme that they name: `incoming`: token rows and feature columns carry different scales.
All inputs are finite; a program needn't handle non-finite values.
Results may differ from the reference program's by a relative error of at most 0.004.
Values may be sent and summed in bfloat16 or wider, within the bound.
No kernel may reach another device: no remote copies, remote signals or barrier semaphores. Data moves between devices by JAX's collectives and lax.ppermute only.
A program may use at most 192 MiB of HBM per device.

```python
import math
import jax
import jax.numpy as jnp
from jax import lax

D = 12288
FFW = 24576
TOKENS = 512
N_SECTION = 2


def draw_incoming(key, part):
    key = jax.random.fold_in(key, 11)
    first, second, third = jax.random.split(key, 3)
    base = jnp.clip(jax.random.normal(first, (N_SECTION, TOKENS, D), jnp.float32), -4.0, 4.0)
    rows = jnp.exp(jax.random.uniform(second, (N_SECTION, TOKENS, 1), jnp.float32, math.log(0.3), math.log(3.0)))
    ramp = jnp.exp(math.log(3.0) * jnp.arange(D, dtype=jnp.float32) / D)
    jitter = jax.random.uniform(third, (N_SECTION, 1, D), jnp.float32, 0.7, 1.0)
    cols = ramp[None, None, :] * jitter / 1.8
    return (base * rows * cols).astype(jnp.bfloat16)


def block_levels(own_key, dims, pieces, low, high):
    loudness, own = 1.0, jax.random.fold_in(own_key, 6)
    for axis_at, blocks in pieces:
        draws = jnp.exp(jax.random.uniform(jax.random.fold_in(own, axis_at), (blocks,), jnp.float32, low / len(pieces), high / len(pieces)))
        loudness = loudness * jnp.repeat(draws, dims[axis_at] // blocks).reshape([-1 if axis == axis_at else 1 for axis in range(len(dims))])
    return loudness


def centred(key, extent, spread, most, cuts=(), held_as=jnp.bfloat16):
    level = block_levels(key, extent, cuts, -0.22, 0.18) if cuts else 1.0
    entries = jax.random.normal(key, extent, jnp.float32) * spread * level
    return jnp.minimum(jnp.maximum(entries, -most), most).astype(held_as)


def setup_inputs(seed: int = 0) -> dict:
    key_of = jax.random.split(jax.random.key(seed), 8)
    incoming = draw_incoming(jax.random.fold_in(key_of[7], 71), 0)
    norm_gain = jnp.clip(1.0 + 0.18 * jax.random.normal(key_of[1], (N_SECTION, D), jnp.float32), 0.1, 1.9)
    norm_shift = centred(key_of[2], (N_SECTION, D), 0.5, 3.0, ((0, 2), (1, 2)), jnp.float32)
    up_weight = centred(key_of[3], (N_SECTION, D, FFW), D ** -0.5, 0.0546875, ((0, 2), (1, 2), (2, 8)))
    up_bias = centred(key_of[4], (N_SECTION, FFW), 1.0, 4.0, ((0, 2), (1, 8)), jnp.float32)
    down_weight = centred(key_of[5], (N_SECTION, FFW, D), FFW ** -0.5, 0.0390625, ((0, 2), (1, 8), (2, 2)))
    down_bias = centred(key_of[6], (N_SECTION, D), 0.5, 3.0, ((0, 2), (1, 2)), jnp.float32)
    return dict(incoming=incoming, norm_gain=norm_gain, norm_shift=norm_shift, up_weight=up_weight, up_bias=up_bias, down_weight=down_weight, down_bias=down_bias)


def sublayer(x_in, gain, shift, up_w, up_b, down_w, down_b):
    x = x_in.astype(jnp.float32)
    total = lax.optimization_barrier(jnp.sum(x, axis=1))
    square = lax.optimization_barrier(jnp.sum(x * x, axis=1))
    mean = total / D
    var = square / D - mean * mean
    normed = ((x - mean[:, None]) * jax.lax.rsqrt(var + 1e-05)[:, None] * gain + shift).astype(jnp.bfloat16)
    pre = jnp.dot(normed, up_w, preferred_element_type=jnp.float32)
    act = jax.nn.gelu(pre + up_b, approximate=True).astype(jnp.bfloat16)
    summed = jnp.dot(act, down_w, preferred_element_type=jnp.float32)
    return (summed + down_b + x).astype(jnp.bfloat16)

def reference(incoming, norm_gain, norm_shift, up_weight, up_bias, down_weight, down_bias):
    outputs = []
    for section in range(N_SECTION):
        outputs.append(sublayer(incoming[section], norm_gain[section], norm_shift[section], up_weight[section], up_bias[section], down_weight[section], down_bias[section]))
    stacked = jnp.stack(outputs)
    return jnp.roll(stacked, 1, axis=0)
```

```python
import jax
import jax.numpy as jnp
from jax import lax
from jax.sharding import PartitionSpec as P

F32 = jnp.float32
BF16 = jnp.bfloat16


def ring_order(n):
    return list(range(0, n, 2)) + list(range(1, n, 2))[::-1]


def make_per_device(width, n_section, n_dp, n_tensor):
    chips = n_tensor // 2
    order = ring_order(chips)
    along = [
        (order[i] * 2 + c, order[(i + 1) % chips] * 2 + c) for i in range(chips) for c in range(2)
    ]
    swap = [(i, i ^ 1) for i in range(n_tensor)]

    def forward(block):
        return lax.ppermute(block, "tensor", along)

    def sibling(block):
        return lax.ppermute(block, "tensor", swap)

    def across(partial_value):
        if n_dp == 1:
            return partial_value
        total = partial_value
        sent = partial_value.astype(BF16)
        for hop in range(1, n_dp):
            route = [(i, (i + hop) % n_dp) for i in range(n_dp)]
            total = total + lax.ppermute(sent, "dp", route).astype(F32)
        return total

    def per_device(incoming, norm_gain, norm_shift, up_weight, up_bias, down_weight, down_bias):
        x = incoming[0].astype(F32)
        up_w = up_weight[0]
        down_w = down_weight[0]
        rows = x.shape[0]
        total, square = lax.psum((jnp.sum(x, axis=1), jnp.sum(x * x, axis=1)), "dp")
        mean = total / width
        var = square / width - mean * mean
        normed = (
            (x - mean[:, None]) * lax.rsqrt(var + 1e-05)[:, None] * norm_gain[0] + norm_shift[0]
        ).astype(BF16)

        parts = []
        block = normed
        for step in range(chips):
            coming = forward(block) if step < chips - 1 else None
            both = jnp.concatenate([block, sibling(block)], axis=0)
            pre = across(jnp.dot(both, up_w, preferred_element_type=F32))
            act = jax.nn.gelu(pre + up_bias[0], approximate=True).astype(BF16)
            parts.append(jnp.dot(act, down_w, preferred_element_type=F32))
            block = coming

        running = None
        for step in list(range(1, chips)) + [0]:
            part = parts[step]
            summed = part[:rows] + sibling(part[rows:].astype(BF16)).astype(F32)
            if running is not None:
                summed = summed + running.astype(F32)
            if step:
                running = forward(summed.astype(BF16))
        result = (summed + down_bias[0] + x).astype(BF16)
        moved = lax.ppermute(
            result, "section", [(i, (i + 1) % n_section) for i in range(n_section)]
        )
        return moved[None]

    return per_device


def solution(mesh):
    placed = (
        P("section", "tensor", "dp"),
        P("section", "dp"),
        P("section", "dp"),
        P("section", "dp", "tensor"),
        P("section", "tensor"),
        P("section", "tensor", "dp"),
        P("section", "dp"),
    )

    def run(*args):
        width = args[0].shape[2]
        body = make_per_device(
            width, mesh.shape["section"], mesh.shape["dp"], mesh.shape["tensor"]
        )
        return jax.shard_map(
            body,
            mesh=mesh,
            in_specs=placed,
            out_specs=P("section", "tensor", "dp"),
            check_vma=False,
        )(*args)

    return run
```

```python
import functools

import jax
import jax.numpy as jnp
from jax import lax
from jax.experimental import pallas as pl
from jax.experimental.pallas import tpu as pltpu
from jax.sharding import PartitionSpec as P

F32 = jnp.float32
BF16 = jnp.bfloat16
MIB = 1024 * 1024
LONG = pl.CostEstimate(flops=20_000_000_000, bytes_accessed=80_000_000, transcendentals=0)


def ring_order(n):
    return list(range(0, n, 2)) + list(range(1, n, 2))[::-1]


def pick_tile(extent, most):
    tile = min(extent, most)
    while extent % tile:
        tile //= 2
    return tile


def sums_kernel(x_ref, out_ref):
    x = x_ref[0].astype(F32)
    total = jnp.sum(x, axis=1, keepdims=True)
    square = jnp.sum(x * x, axis=1, keepdims=True)
    lane = lax.broadcasted_iota(jnp.int32, out_ref.shape, 1)
    out_ref[...] = jnp.where(lane == 0, total, square)


def row_sums(incoming):
    rows = incoming.shape[1]
    return pl.pallas_call(
        sums_kernel,
        out_shape=jax.ShapeDtypeStruct((rows, 128), F32),
        compiler_params=pltpu.CompilerParams(vmem_limit_bytes=16 * MIB),
    )(incoming)


def up_kernel(width, n_dp, n_tensor, at_ref, a_ref, b_ref, sums_ref, gain_ref, shift_ref, w_ref, *rest):
    wide_ref, sent_ref, normed_ref = rest[-3:]
    rows = a_ref.shape[0]

    @pl.when(pl.program_id(0) == 0)
    def _():
        for half, block_ref in enumerate((a_ref, b_ref)):
            sums = jnp.zeros((rows, 128), F32)
            for k in range(n_dp):
                start = pl.multiple_of((at_ref[half] + k * n_tensor) * rows, rows)
                sums = sums + sums_ref[pl.ds(start, rows), :]
            mean = sums[:, 0:1] / width
            var = sums[:, 1:2] / width - mean * mean
            scale = lax.rsqrt(var + 1e-05)
            x = block_ref[...].astype(F32)
            normed_ref[half * rows : (half + 1) * rows, :] = (
                (x - mean) * scale * gain_ref[...] + shift_ref[...]
            ).astype(BF16)

    product = jnp.dot(normed_ref[...], w_ref[0], preferred_element_type=F32)
    wide_ref[...] = product
    sent_ref[...] = product.astype(BF16)


def up_product(width, n_dp, n_tensor, at, a, b, sums, gain, shift, weight, after):
    rows, depth = a.shape
    columns = weight.shape[2]
    tile = pick_tile(columns, 256)
    whole = lambda shape: pl.BlockSpec(shape, lambda j, at: (0,) * len(shape))
    out = pl.BlockSpec((2 * rows, tile), lambda j, at: (0, j))
    return pl.pallas_call(
        functools.partial(up_kernel, width, n_dp, n_tensor),
        out_shape=(
            jax.ShapeDtypeStruct((2 * rows, columns), F32),
            jax.ShapeDtypeStruct((2 * rows, columns), BF16),
        ),
        grid_spec=pltpu.PrefetchScalarGridSpec(
            num_scalar_prefetch=1,
            grid=(columns // tile,),
            in_specs=[
                whole(a.shape),
                whole(b.shape),
                whole(sums.shape),
                whole(gain.shape),
                whole(shift.shape),
                pl.BlockSpec((1, depth, tile), lambda j, at: (0, 0, j)),
            ]
            + [pl.BlockSpec(memory_space=pl.ANY)] * len(after),
            out_specs=[out, out],
            scratch_shapes=[pltpu.VMEM((2 * rows, depth), BF16)],
        ),
        compiler_params=pltpu.CompilerParams(vmem_limit_bytes=28 * MIB),
        cost_estimate=LONG,
    )(at, a, b, sums, gain, shift, weight, *after)


def down_kernel(own_ref, other_ref, bias_ref, w_ref, *rest):
    mine_ref, theirs_ref, total_ref = rest[-3:]
    rows = mine_ref.shape[0]
    step = pl.program_id(0)
    pre = own_ref[...] + other_ref[...].astype(F32) + bias_ref[...]
    act = jax.nn.gelu(pre, approximate=True).astype(BF16)
    product = jnp.dot(act, w_ref[0], preferred_element_type=F32)

    @pl.when(step == 0)
    def _():
        total_ref[...] = product

    @pl.when(step > 0)
    def _():
        total_ref[...] += product

    @pl.when(step == pl.num_programs(0) - 1)
    def _():
        mine_ref[...] = total_ref[:rows, :]
        theirs_ref[...] = total_ref[rows:, :].astype(BF16)


def down_product(own, other, bias, weight, after):
    rows = own.shape[0] // 2
    depth, columns = weight.shape[1:]
    tile = pick_tile(depth, 256)
    return pl.pallas_call(
        down_kernel,
        out_shape=(
            jax.ShapeDtypeStruct((rows, columns), F32),
            jax.ShapeDtypeStruct((rows, columns), BF16),
        ),
        grid=(depth // tile,),
        in_specs=[
            pl.BlockSpec((2 * rows, tile), lambda k: (0, k)),
            pl.BlockSpec((2 * rows, tile), lambda k: (0, k)),
            pl.BlockSpec((1, tile), lambda k: (0, k)),
            pl.BlockSpec((1, tile, columns), lambda k: (0, k, 0)),
        ]
        + [pl.BlockSpec(memory_space=pl.ANY)] * len(after),
        out_specs=[pl.BlockSpec((rows, columns), lambda k: (0, 0))] * 2,
        scratch_shapes=[pltpu.VMEM((2 * rows, columns), F32)],
        compiler_params=pltpu.CompilerParams(vmem_limit_bytes=28 * MIB),
        cost_estimate=LONG,
    )(own, other, bias, weight, *after)


def make_per_device(width, n_section, n_dp, n_tensor):
    chips = n_tensor // 2
    order = ring_order(chips)
    along = [
        (order[i] * 2 + c, order[(i + 1) % chips] * 2 + c) for i in range(chips) for c in range(2)
    ]
    swap = [(i, i ^ 1) for i in range(n_tensor)]
    source = [
        [
            [order[(order.index(t // 2) - k) % chips] * 2 + (t % 2 ^ half) for half in range(2)]
            for t in range(n_tensor)
        ]
        for k in range(chips)
    ]

    def forward(block):
        return lax.ppermute(block, "tensor", along)

    def sibling(block):
        return lax.ppermute(block, "tensor", swap)

    def from_others(sent):
        total = None
        for hop in range(1, n_dp):
            route = [(i, (i + hop) % n_dp) for i in range(n_dp)]
            got = lax.ppermute(sent, "dp", route)
            total = got if total is None else total.astype(F32) + got.astype(F32)
        return total

    def per_device(incoming, norm_gain, norm_shift, up_weight, up_bias, down_weight, down_bias):
        rows = incoming.shape[1]
        raw = incoming[0]
        me = lax.axis_index("tensor")
        at = jnp.asarray(source, jnp.int32)[:, me]
        sums = lax.all_gather(row_sums(incoming), ("dp", "tensor"), axis=0, tiled=True)

        blocks, siblings = [raw], [sibling(raw)]

        pres, parts = {}, {}
        last = ()

        def up(k):
            nonlocal last
            coming = forward(blocks[k]) if k < chips - 1 else None
            wide, sent = up_product(
                width, n_dp, n_tensor, at[k], blocks[k], siblings[k], sums,
                norm_gain, norm_shift, up_weight, last,
            )
            if coming is not None:
                coming, wide = lax.optimization_barrier((coming, wide))
                blocks.append(coming)
                siblings.append(sibling(coming))
            pres[k] = (wide, from_others(sent))
            last = (wide,)

        def down(k):
            nonlocal last
            mine, theirs = down_product(*pres[k], up_bias, down_weight, last)
            last = (mine,)
            if k == 1:
                first = (mine + sibling(theirs).astype(F32)).astype(BF16)
                running.append(forward(first))
                last = (first,)
            else:
                parts[k] = (mine, sibling(theirs))

        running = []
        up(0)
        if chips > 1:
            up(1)
        for k in range(2, chips):
            up(k)
            down(k - 1)
        if chips > 1:
            down(chips - 1)
        down(0)

        for k in list(range(2, chips)) + [0]:
            mine, got = parts[k]
            summed = mine + got.astype(F32)
            if running:
                summed = summed + running[-1].astype(F32)
            if k:
                running.append(forward(summed.astype(BF16)))
        result = (summed + down_bias[0] + raw.astype(F32)).astype(BF16)
        moved = lax.ppermute(
            result, "section", [(i, (i + 1) % n_section) for i in range(n_section)]
        )
        return moved[None]

    return per_device


def solution(mesh):
    placed = (
        P("section", "tensor", "dp"),
        P("section", "dp"),
        P("section", "dp"),
        P("section", "dp", "tensor"),
        P("section", "tensor"),
        P("section", "tensor", "dp"),
        P("section", "dp"),
    )

    def run(*args):
        body = make_per_device(
            args[0].shape[2], mesh.shape["section"], mesh.shape["dp"], mesh.shape["tensor"]
        )
        return jax.shard_map(
            body,
            mesh=mesh,
            in_specs=placed,
            out_specs=P("section", "tensor", "dp"),
            check_vma=False,
        )(*args)

    return run
```

```python
import jax
import jax.numpy as jnp
from jax import lax
from jax.sharding import PartitionSpec as P

F32 = jnp.float32
BF16 = jnp.bfloat16


def ring_order(n):
    return list(range(0, n, 2)) + list(range(1, n, 2))[::-1]


def make_per_device(width, n_section, n_dp, n_tensor):
    chips = n_tensor // 2
    order = ring_order(chips)
    along = [
        (order[i] * 2 + c, order[(i + 1) % chips] * 2 + c) for i in range(chips) for c in range(2)
    ]
    swap = [(i, i ^ 1) for i in range(n_tensor)]
    turn = [(i, (i + 1) % n_section) for i in range(n_section)]
    along_and_turn = [
        (s * n_tensor + a, t * n_tensor + b) for s, t in turn for a, b in along
    ]

    def forward(block):
        return lax.ppermute(block, "tensor", along)

    def sibling(block):
        return lax.ppermute(block, "tensor", swap)

    def from_others(sent):
        total = None
        for hop in range(1, n_dp):
            route = [(i, (i + hop) % n_dp) for i in range(n_dp)]
            got = lax.ppermute(sent, "dp", route)
            total = got if total is None else total.astype(F32) + got.astype(F32)
        return total

    def per_device(incoming, norm_gain, norm_shift, up_weight, up_bias, down_weight, down_bias):
        rows = incoming.shape[1]
        x = incoming[0].astype(F32)
        sums = jnp.stack(
            lax.reduce(
                (x, x * x), (F32(0), F32(0)), lambda a, b: (a[0] + b[0], a[1] + b[1]), (1,)
            )
        )
        total, square = sums + from_others(sums)
        mean = total / width
        var = square / width - mean * mean
        normed = (
            (x - mean[:, None]) * lax.rsqrt(var + 1e-05)[:, None] * norm_gain[0] + norm_shift[0]
        ).astype(BF16)

        blocks, pres = [(normed, sibling(normed))], []

        def tie(values, done):
            return lax.optimization_barrier((values, done))[0]

        def up(k):
            block = blocks[k][0]
            coming = forward(block) if k < chips - 1 else None
            both = jnp.concatenate(blocks[k], axis=0)
            pre = jnp.dot(both, up_weight[0], preferred_element_type=F32)
            other = from_others(pre.astype(BF16))
            if coming is not None:
                coming = tie(coming, pre)
                blocks.append((coming, sibling(coming)))
            pres.append((pre, other))
            return pre

        def act(k, done):
            pre, other = pres[k]
            if done is not None:
                other = tie(other, done)
            return jax.nn.gelu(pre + other.astype(F32) + up_bias[0], approximate=True).astype(BF16)

        def send(k, value):
            if k < chips - 1:
                return forward(value)
            return lax.ppermute(value, ("section", "tensor"), along_and_turn)

        up(0)
        residual = lax.ppermute(incoming[0], "section", turn)
        for k in range(1, chips):
            if k == 1:
                blocks[1] = tie(blocks[1], residual)
                up(1)
                done = (pres[1][0], pres[0][1])
                if chips > 2:
                    blocks[2] = tie(blocks[2], done)
                    done = up(2)
                both = jnp.concatenate([act(1, done), act(0, None)], axis=0)
                part = jnp.dot(both, down_weight[0], preferred_element_type=F32)
                if chips > 2:
                    part = tie(part, pres[2][1])
                got = sibling(part[rows : 2 * rows].astype(BF16))
                summed = (part[:rows] + got.astype(F32)).astype(BF16)
                running = send(1, summed)
                own = part[2 * rows : 3 * rows] + sibling(part[3 * rows :].astype(BF16)).astype(F32)
                own = lax.ppermute((own + down_bias[0]).astype(BF16), "section", turn)
                continue
            if k + 1 < chips:
                blocks[k + 1] = tie(blocks[k + 1], summed)
                done = (up(k + 1), running, own)
            else:
                done = summed
            part = jnp.dot(act(k, done), down_weight[0], preferred_element_type=F32)
            part = tie(part, pres[k + 1][1] if k + 1 < chips else running)
            got = sibling(part[rows:].astype(BF16))
            summed = (part[:rows] + got.astype(F32) + running.astype(F32)).astype(BF16)
            running = send(k, summed)
        result = running.astype(F32) + own.astype(F32) + residual.astype(F32)
        return result.astype(BF16)[None]

    return per_device


def solution(mesh):
    placed = (
        P("section", "tensor", "dp"),
        P("section", "dp"),
        P("section", "dp"),
        P("section", "dp", "tensor"),
        P("section", "tensor"),
        P("section", "tensor", "dp"),
        P("section", "dp"),
    )

    def run(*args):
        body = make_per_device(
            args[0].shape[2], mesh.shape["section"], mesh.shape["dp"], mesh.shape["tensor"]
        )
        return jax.shard_map(
            body,
            mesh=mesh,
            in_specs=placed,
            out_specs=P("section", "tensor", "dp"),
            check_vma=False,
        )(*args)

    return run
```

```python
import jax
import jax.numpy as jnp
from jax import lax
from jax.sharding import PartitionSpec as P

F32 = jnp.float32
BF16 = jnp.bfloat16


def ring_order(n):
    return list(range(0, n, 2)) + list(range(1, n, 2))[::-1]


def make_per_device(width, n_section, n_dp, n_tensor):
    chips = n_tensor // 2
    order = ring_order(chips)
    along = [
        (order[i] * 2 + c, order[(i + 1) % chips] * 2 + c) for i in range(chips) for c in range(2)
    ]
    swap = [(i, i ^ 1) for i in range(n_tensor)]
    turn = [(i, (i + 1) % n_section) for i in range(n_section)]
    along_and_turn = [
        (s * n_tensor + a, t * n_tensor + b) for s, t in turn for a, b in along
    ]

    def forward(block):
        return lax.ppermute(block, "tensor", along)

    def sibling(block):
        return lax.ppermute(block, "tensor", swap)

    def from_others(sent):
        total = None
        for hop in range(1, n_dp):
            route = [(i, (i + hop) % n_dp) for i in range(n_dp)]
            got = lax.ppermute(sent, "dp", route)
            total = got if total is None else total.astype(F32) + got.astype(F32)
        return total

    def per_device(incoming, norm_gain, norm_shift, up_weight, up_bias, down_weight, down_bias):
        rows = incoming.shape[1]
        x = incoming[0].astype(F32)
        sums = jnp.stack(
            lax.reduce(
                (x, x * x), (F32(0), F32(0)), lambda a, b: (a[0] + b[0], a[1] + b[1]), (1,)
            )
        )
        total, square = sums + from_others(sums)
        mean = total / width
        var = square / width - mean * mean
        normed = (
            (x - mean[:, None]) * lax.rsqrt(var + 1e-05)[:, None] * norm_gain[0] + norm_shift[0]
        ).astype(BF16)

        blocks, pres = [(normed, sibling(normed))], []

        def tie(values, done):
            return lax.optimization_barrier((values, done))[0]

        def up(k):
            block = blocks[k][0]
            coming = forward(block) if k < chips - 1 else None
            both = jnp.concatenate(blocks[k], axis=0)
            pre = jnp.dot(both, up_weight[0], preferred_element_type=F32)
            other = from_others(pre.astype(BF16))
            if coming is not None:
                coming = tie(coming, (pre, pres[0][1]) if k == 1 else pre)
                blocks.append((coming, sibling(coming)))
            pres.append((pre, other))
            return pre

        def act(k, done):
            pre, other = pres[k]
            if done is not None:
                other = tie(other, done)
            return jax.nn.gelu(pre + other.astype(F32) + up_bias[0], approximate=True).astype(BF16)

        def send(k, value):
            if k < chips - 1:
                return forward(value)
            return lax.ppermute(value, ("section", "tensor"), along_and_turn)

        up(0)
        residual = lax.ppermute(tie(incoming[0], pres[0][0]), "section", turn)
        for k in range(1, chips):
            if k == 1:
                up(1)
                done = (pres[1][0], pres[0][1], residual)
                if chips > 2:
                    blocks[2] = tie(blocks[2], done)
                    done = up(2)
                both = jnp.concatenate([act(1, done), act(0, None)], axis=0)
                part = jnp.dot(both, down_weight[0], preferred_element_type=F32)
                theirs = part[rows : 2 * rows].astype(BF16)
                if chips > 2:
                    theirs = tie(theirs, pres[2][1])
                summed = (part[:rows] + sibling(theirs).astype(F32)).astype(BF16)
                running = send(1, summed)
                theirs = tie(part[3 * rows :].astype(BF16), summed)
                own = part[2 * rows : 3 * rows] + sibling(theirs).astype(F32)
                own = lax.ppermute((own + down_bias[0]).astype(BF16), "section", turn)
                continue
            if k + 1 < chips:
                blocks[k + 1] = tie(blocks[k + 1], summed)
                done = (up(k + 1), running)
            else:
                done = summed
            part = jnp.dot(act(k, done), down_weight[0], preferred_element_type=F32)
            theirs = part[rows:].astype(BF16)
            theirs = tie(theirs, pres[k + 1][1] if k + 1 < chips else (running, own))
            summed = part[:rows] + sibling(theirs).astype(F32) + running.astype(F32)
            summed = summed.astype(BF16)
            running = send(k, summed)
        result = running.astype(F32) + own.astype(F32) + residual.astype(F32)
        return result.astype(BF16)[None]

    return per_device


def solution(mesh):
    placed = (
        P("section", "tensor", "dp"),
        P("section", "dp"),
        P("section", "dp"),
        P("section", "dp", "tensor"),
        P("section", "tensor"),
        P("section", "tensor", "dp"),
        P("section", "dp"),
    )

    def run(*args):
        body = make_per_device(
            args[0].shape[2], mesh.shape["section"], mesh.shape["dp"], mesh.shape["tensor"]
        )
        return jax.shard_map(
            body,
            mesh=mesh,
            in_specs=placed,
            out_specs=P("section", "tensor", "dp"),
            check_vma=False,
        )(*args)

    return run
```

```python
import jax
import jax.numpy as jnp
from jax import lax
from jax.sharding import PartitionSpec as P

F32 = jnp.float32
BF16 = jnp.bfloat16


def ring_order(n):
    return list(range(0, n, 2)) + list(range(1, n, 2))[::-1]


def make_per_device(width, n_section, n_dp, n_tensor):
    chips = n_tensor // 2
    order = ring_order(chips)
    ahead = chips // 2
    swap = [(i, i ^ 1) for i in range(n_tensor)]
    turn = [(i, (i + 1) % n_section) for i in range(n_section)]

    def hops(way):
        return [
            (order[i] * 2 + c, order[(i + way) % chips] * 2 + c)
            for i in range(chips)
            for c in range(2)
        ]

    def shift(block, way):
        return lax.ppermute(block, "tensor", hops(way))

    def shift_and_turn(block, way):
        route = [(s * n_tensor + a, t * n_tensor + b) for s, t in turn for a, b in hops(way)]
        return lax.ppermute(block, ("section", "tensor"), route)

    def sibling(block):
        return lax.ppermute(block, "tensor", swap)

    def from_others(sent):
        total = None
        for hop in range(1, n_dp):
            route = [(i, (i + hop) % n_dp) for i in range(n_dp)]
            got = lax.ppermute(sent, "dp", route)
            total = got if total is None else total.astype(F32) + got.astype(F32)
        return total

    def per_device(incoming, norm_gain, norm_shift, up_weight, up_bias, down_weight, down_bias):
        rows = incoming.shape[1]
        x = incoming[0].astype(F32)
        sums = jnp.stack(
            lax.reduce(
                (x, x * x), (F32(0), F32(0)), lambda a, b: (a[0] + b[0], a[1] + b[1]), (1,)
            )
        )
        total, square = sums + from_others(sums)
        mean = total / width
        var = square / width - mean * mean
        normed = (
            (x - mean[:, None]) * lax.rsqrt(var + 1e-05)[:, None] * norm_gain[0] + norm_shift[0]
        ).astype(BF16)

        pres = {}

        def tie(values, done):
            return lax.optimization_barrier((values, done))[0]

        def up(offset, block):
            both = jnp.concatenate([block, sibling(block)], axis=0)
            pre = jnp.dot(both, up_weight[0], preferred_element_type=F32)
            pres[offset] = (pre, from_others(pre.astype(BF16)))
            return pre

        def act(offset, done=None):
            pre, other = pres[offset]
            if done is not None:
                other = tie(other, done)
            return jax.nn.gelu(pre + other.astype(F32) + up_bias[0], approximate=True).astype(BF16)

        ups = [(chips - k, 1) for k in range(1, ahead + 1)]
        ups += [(k, -1) for k in range(1, chips - ahead)]
        done = up(0, normed)
        residual = lax.ppermute(tie(incoming[0], done), "section", turn)
        carried, before = {1: normed, -1: normed}, None
        for offset, way in ups:
            block = shift(carried[way], way)
            extra = () if before is None else (pres[before][1], residual)
            block = tie(block, (done, extra))
            carried[way] = block
            before = 0 if before is None else last
            last = offset
            done = up(offset, block)

        along = [(k, 1) for k in range(ahead, 0, -1)]
        against = [(chips - k, -1) for k in range(chips - ahead - 1, 0, -1)]
        downs = [along.pop(0)]
        while along or against:
            downs.append(against.pop(0) if against else along.pop(0))
            if along and len(downs) % 2 == 0:
                downs.append(along.pop(0))

        sums, arrived = {}, []
        own = sent = None
        for place, (offset, way) in enumerate(downs):
            active = act(offset, done)
            if place == 0:
                mine = act(0)
                active = jnp.concatenate(
                    [active[:rows], mine[:rows], active[rows:], mine[rows:]], axis=0
                )
            part = jnp.dot(active, down_weight[0], preferred_element_type=F32)
            half = part.shape[0] // 2
            theirs = part[half:].astype(BF16)
            if place:
                over = pres[downs[place + 1][0]][1] if place + 1 < len(downs) else ()
                theirs = tie(theirs, (sent, over, own))
            got = sibling(theirs)
            summed = part[:rows] + got[:rows].astype(F32)
            if way in sums:
                summed = summed + sums[way].astype(F32)
            summed = summed.astype(BF16)
            if offset == way % chips:
                sent = shift_and_turn(summed, way)
                arrived.append(sent)
            else:
                sent = sums[way] = shift(summed, way)
            done = summed
            if place == 0:
                own = (part[rows:half] + got[rows:].astype(F32) + down_bias[0]).astype(BF16)
                done = (summed, own)
                own = lax.ppermute(own, "section", turn)
        result = own.astype(F32) + residual.astype(F32)
        for value in arrived:
            result = result + value.astype(F32)
        return result.astype(BF16)[None]

    return per_device


def solution(mesh):
    placed = (
        P("section", "tensor", "dp"),
        P("section", "dp"),
        P("section", "dp"),
        P("section", "dp", "tensor"),
        P("section", "tensor"),
        P("section", "tensor", "dp"),
        P("section", "dp"),
    )

    def run(*args):
        body = make_per_device(
            args[0].shape[2], mesh.shape["section"], mesh.shape["dp"], mesh.shape["tensor"]
        )
        return jax.shard_map(
            body,
            mesh=mesh,
            in_specs=placed,
            out_specs=P("section", "tensor", "dp"),
            check_vma=False,
        )(*args)

    return run
```

```python
import jax
import jax.numpy as jnp
from jax import lax
from jax.sharding import PartitionSpec as P

F32 = jnp.float32
BF16 = jnp.bfloat16


def ring_order(n):
    return list(range(0, n, 2)) + list(range(1, n, 2))[::-1]


def make_per_device(width, n_section, n_dp, n_tensor):
    chips = n_tensor // 2
    order = ring_order(chips)
    ahead = chips // 2
    swap = [(i, i ^ 1) for i in range(n_tensor)]
    turn = [(i, (i + 1) % n_section) for i in range(n_section)]

    def hops(way):
        return [
            (order[i] * 2 + c, order[(i + way) % chips] * 2 + c)
            for i in range(chips)
            for c in range(2)
        ]

    def shift(block, way):
        return lax.ppermute(block, "tensor", hops(way))

    def shift_and_turn(block, way):
        route = [(s * n_tensor + a, t * n_tensor + b) for s, t in turn for a, b in hops(way)]
        return lax.ppermute(block, ("section", "tensor"), route)

    def sibling(block):
        return lax.ppermute(block, "tensor", swap)

    def from_others(sent):
        total = None
        for hop in range(1, n_dp):
            route = [(i, (i + hop) % n_dp) for i in range(n_dp)]
            got = lax.ppermute(sent, "dp", route)
            total = got if total is None else total.astype(F32) + got.astype(F32)
        return total

    def per_device(incoming, norm_gain, norm_shift, up_weight, up_bias, down_weight, down_bias):
        rows = incoming.shape[1]
        x = incoming[0].astype(F32)
        sums = jnp.stack(
            lax.reduce(
                (x, x * x), (F32(0), F32(0)), lambda a, b: (a[0] + b[0], a[1] + b[1]), (1,)
            )
        )
        total, square = sums + from_others(sums)
        mean = total / width
        var = square / width - mean * mean
        normed = (
            (x - mean[:, None]) * lax.rsqrt(var + 1e-05)[:, None] * norm_gain[0] + norm_shift[0]
        ).astype(BF16)

        pres = {}

        def tie(values, done):
            return lax.optimization_barrier((values, done))[0]

        def up(held):
            both = jnp.concatenate([half for block in held for half in (block, sibling(block))])
            return jnp.dot(both, up_weight[0], preferred_element_type=F32)

        def act(offset, done):
            pre, other = pres[offset]
            other = tie(other, done)
            return jax.nn.gelu(pre + other.astype(F32) + up_bias[0], approximate=True).astype(BF16)

        def down(offset, done, over):
            part = jnp.dot(act(offset, done), down_weight[0], preferred_element_type=F32)
            theirs = tie(part[rows:].astype(BF16), over)
            return part[:rows] + sibling(theirs).astype(F32)

        pre = up([normed])
        pres[0] = (pre, from_others(pre.astype(BF16)))
        block = tie(shift(normed, 1), pre)
        ahead_blocks, back_blocks = {}, {}
        back = tie(normed, pre)
        for k in range(1, chips - ahead):
            back_blocks[k] = back = shift(back, -1)
        pre = up([block])
        front = tie(block, pre)
        for k in range(2, ahead + 1):
            ahead_blocks[chips - k] = front = shift(front, 1)
        pres[chips - 1] = (pre, from_others(pre.astype(BF16)))
        residual = lax.ppermute(tie(incoming[0], pre), "section", turn)

        own = down(0, (pre, back_blocks), (ahead_blocks, pres[chips - 1][1], residual))
        own = (own + down_bias[0]).astype(BF16)
        done = own
        own = lax.ppermute(own, "section", turn)

        along = [(k, 1) for k in range(ahead, 0, -1)]
        against = [(chips - k, -1) for k in range(chips - ahead - 1, 0, -1)]
        downs = []
        while along or against:
            for offsets in (against, along):
                if offsets:
                    downs.append(offsets.pop(0))
        held = {**ahead_blocks, **back_blocks}
        rest = [offset for offset, _ in downs if offset in held]
        if rest:
            held = tie(held, done)
            done = pre = up([held[offset] for offset in rest])
            for place, offset in enumerate(rest):
                pres[offset] = (pre[2 * rows * place : 2 * rows * (place + 1)], None)

        def exchange(place, done=None):
            if place < len(downs):
                pre, other = pres[downs[place][0]]
                if other is None:
                    sent = pre.astype(BF16)
                    other = from_others(sent if done is None else tie(sent, done))
                    pres[downs[place][0]] = (pre, other)
                return other
            return ()

        exchange(0)
        coming = exchange(1)
        sums, arrived, over = {}, [], own
        for place, (offset, way) in enumerate(downs):
            summed = down(offset, done, (over, coming))
            if way in sums:
                summed = summed + sums[way].astype(F32)
            done = summed = summed.astype(BF16)
            if offset == way % chips:
                over = shift_and_turn(summed, way)
                arrived.append(over)
            else:
                over = sums[way] = shift(summed, way)
            coming = exchange(place + 2, summed)
        result = own.astype(F32) + residual.astype(F32)
        for value in arrived:
            result = result + value.astype(F32)
        return result.astype(BF16)[None]

    return per_device


def solution(mesh):
    placed = (
        P("section", "tensor", "dp"),
        P("section", "dp"),
        P("section", "dp"),
        P("section", "dp", "tensor"),
        P("section", "tensor"),
        P("section", "tensor", "dp"),
        P("section", "dp"),
    )

    def run(*args):
        body = make_per_device(
            args[0].shape[2], mesh.shape["section"], mesh.shape["dp"], mesh.shape["tensor"]
        )
        return jax.shard_map(
            body,
            mesh=mesh,
            in_specs=placed,
            out_specs=P("section", "tensor", "dp"),
            check_vma=False,
        )(*args)

    return run
```

```python
import jax
import jax.numpy as jnp
from jax import lax
from jax.sharding import PartitionSpec as P

F32 = jnp.float32
BF16 = jnp.bfloat16


def ring_order(n):
    return list(range(0, n, 2)) + list(range(1, n, 2))[::-1]


def make_per_device(width, n_section, n_dp, n_tensor):
    chips = n_tensor // 2
    order = ring_order(chips)
    ahead = chips // 2
    swap = [(i, i ^ 1) for i in range(n_tensor)]
    turn = [(i, (i + 1) % n_section) for i in range(n_section)]

    def hops(way):
        return [
            (order[i] * 2 + c, order[(i + way) % chips] * 2 + c)
            for i in range(chips)
            for c in range(2)
        ]

    def shift(block, way):
        return lax.ppermute(block, "tensor", hops(way))

    def shift_and_turn(block, way):
        route = [(s * n_tensor + a, t * n_tensor + b) for s, t in turn for a, b in hops(way)]
        return lax.ppermute(block, ("section", "tensor"), route)

    def sibling(block):
        return lax.ppermute(block, "tensor", swap)

    def from_others(sent):
        total = None
        for hop in range(1, n_dp):
            route = [(i, (i + hop) % n_dp) for i in range(n_dp)]
            got = lax.ppermute(sent, "dp", route)
            total = got if total is None else total.astype(F32) + got.astype(F32)
        return total

    def per_device(incoming, norm_gain, norm_shift, up_weight, up_bias, down_weight, down_bias):
        rows = incoming.shape[1]
        x = incoming[0].astype(F32)
        sums = jnp.stack(
            lax.reduce(
                (x, x * x), (F32(0), F32(0)), lambda a, b: (a[0] + b[0], a[1] + b[1]), (1,)
            )
        )
        total, square = sums + from_others(sums)
        mean = total / width
        var = square / width - mean * mean
        normed = (
            (x - mean[:, None]) * lax.rsqrt(var + 1e-05)[:, None] * norm_gain[0] + norm_shift[0]
        ).astype(BF16)

        pres = {}

        def tie(values, done):
            return lax.optimization_barrier((values, done))[0]

        def up(held):
            both = jnp.concatenate([half for block in held for half in (block, sibling(block))])
            return jnp.dot(both, up_weight[0], preferred_element_type=F32)

        def act(offset, done):
            pre, other = pres[offset]
            other = tie(other, done)
            return jax.nn.gelu(pre + other.astype(F32) + up_bias[0], approximate=True).astype(BF16)

        def down(offset, done, over):
            part = jnp.dot(act(offset, done), down_weight[0], preferred_element_type=F32)
            theirs = tie(part[rows:].astype(BF16), over)
            return part[:rows] + sibling(theirs).astype(F32), theirs

        pre = up([normed])
        pres[0] = (pre, from_others(pre.astype(BF16)))
        block = tie(shift(normed, 1), pre)
        ahead_blocks, back_blocks = {}, {}
        back = tie(normed, pre)
        for k in range(1, chips - ahead):
            back_blocks[k] = back = shift(back, -1)
        pre = up([block])
        front = tie(block, pre)
        for k in range(2, ahead + 1):
            ahead_blocks[chips - k] = front = shift(front, 1)
        pres[chips - 1] = (pre, from_others(pre.astype(BF16)))
        own, done = down(0, (pre, back_blocks), (ahead_blocks, pres[chips - 1][1]))
        own = lax.ppermute((own + down_bias[0] + x).astype(BF16), "section", turn)

        along = [(k, 1) for k in range(ahead, 0, -1)]
        against = [(chips - k, -1) for k in range(chips - ahead - 1, 0, -1)]
        downs = []
        while along or against:
            for offsets in (against, along):
                if offsets:
                    downs.append(offsets.pop(0))
        held = {**ahead_blocks, **back_blocks}
        rest = [offset for offset, _ in downs if offset in held]
        if rest:
            held = tie(held, done)
            done = pre = up([held[offset] for offset in rest])
            for place, offset in enumerate(rest):
                pres[offset] = (pre[2 * rows * place : 2 * rows * (place + 1)], None)

        def exchange(place, done=None):
            if place < len(downs):
                pre, other = pres[downs[place][0]]
                if other is None:
                    sent = pre.astype(BF16)
                    other = from_others(sent if done is None else tie(sent, done))
                    pres[downs[place][0]] = (pre, other)
                return other
            return ()

        exchange(0)
        coming = exchange(1)
        sums, arrived, over = {}, [], own
        for place, (offset, way) in enumerate(downs):
            summed, _ = down(offset, done, (over, coming))
            if way in sums:
                summed = summed + sums[way].astype(F32)
            done = summed = summed.astype(BF16)
            if offset == way % chips:
                over = shift_and_turn(summed, way)
                arrived.append(over)
            else:
                over = sums[way] = shift(summed, way)
            coming = exchange(place + 2, coming)
        result = own.astype(F32)
        for value in arrived:
            result = result + value.astype(F32)
        return result.astype(BF16)[None]

    return per_device


def solution(mesh):
    placed = (
        P("section", "tensor", "dp"),
        P("section", "dp"),
        P("section", "dp"),
        P("section", "dp", "tensor"),
        P("section", "tensor"),
        P("section", "tensor", "dp"),
        P("section", "dp"),
    )

    def run(*args):
        body = make_per_device(
            args[0].shape[2], mesh.shape["section"], mesh.shape["dp"], mesh.shape["tensor"]
        )
        return jax.shard_map(
            body,
            mesh=mesh,
            in_specs=placed,
            out_specs=P("section", "tensor", "dp"),
            check_vma=False,
        )(*args)

    return run
```

```python
import jax
import jax.numpy as jnp
from jax import lax
from jax.sharding import PartitionSpec as P

F32 = jnp.float32
BF16 = jnp.bfloat16


def ring_order(n):
    return list(range(0, n, 2)) + list(range(1, n, 2))[::-1]


def make_per_device(width, n_section, n_dp, n_tensor):
    chips = n_tensor // 2
    order = ring_order(chips)
    along = [
        (order[i] * 2 + c, order[(i + 1) % chips] * 2 + c) for i in range(chips) for c in range(2)
    ]
    swap = [(i, i ^ 1) for i in range(n_tensor)]
    turn = [(i, (i + 1) % n_section) for i in range(n_section)]
    along_and_turn = [
        (s * n_tensor + a, t * n_tensor + b) for s, t in turn for a, b in along
    ]

    def forward(block):
        return lax.ppermute(block, "tensor", along)

    def sibling(block):
        return lax.ppermute(block, "tensor", swap)

    def from_others(sent):
        total = None
        for hop in range(1, n_dp):
            route = [(i, (i + hop) % n_dp) for i in range(n_dp)]
            got = lax.ppermute(sent, "dp", route)
            total = got if total is None else total.astype(F32) + got.astype(F32)
        return total

    def per_device(incoming, norm_gain, norm_shift, up_weight, up_bias, down_weight, down_bias):
        rows = incoming.shape[1]
        x = incoming[0].astype(F32)
        sums = jnp.stack(
            lax.reduce(
                (x, x * x), (F32(0), F32(0)), lambda a, b: (a[0] + b[0], a[1] + b[1]), (1,)
            )
        )
        total, square = sums + from_others(sums)
        mean = total / width
        var = square / width - mean * mean
        normed = (
            (x - mean[:, None]) * lax.rsqrt(var + 1e-05)[:, None] * norm_gain[0] + norm_shift[0]
        ).astype(BF16)

        blocks, pres = [(normed, sibling(normed))], []

        def tie(values, done):
            return lax.optimization_barrier((values, done))[0]

        def up(k):
            block = blocks[k][0]
            coming = forward(block) if k < chips - 1 else None
            both = jnp.concatenate(blocks[k], axis=0)
            pre = jnp.dot(both, up_weight[0], preferred_element_type=F32)
            other = from_others(pre.astype(BF16))
            if coming is not None:
                coming = tie(coming, (pre, pres[0][1]) if k == 1 else pre)
                blocks.append((coming, sibling(coming)))
            pres.append((pre, other))
            return pre

        def act(k, done):
            pre, other = pres[k]
            if done is not None:
                other = tie(other, done)
            return jax.nn.gelu(pre + other.astype(F32) + up_bias[0], approximate=True).astype(BF16)

        def send(k, value):
            if k < chips - 1:
                return forward(value)
            return lax.ppermute(value, ("section", "tensor"), along_and_turn)

        up(0)
        for k in range(1, chips):
            if k == 1:
                up(1)
                done = (pres[1][0], pres[0][1])
                if chips > 2:
                    blocks[2] = tie(blocks[2], done)
                    done = up(2)
                both = jnp.concatenate([act(1, done), act(0, None)], axis=0)
                part = jnp.dot(both, down_weight[0], preferred_element_type=F32)
                theirs = part[rows : 2 * rows].astype(BF16)
                if chips > 2:
                    theirs = tie(theirs, pres[2][1])
                summed = (part[:rows] + sibling(theirs).astype(F32)).astype(BF16)
                running = send(1, summed)
                theirs = tie(part[3 * rows :].astype(BF16), summed)
                mine, got = part[2 * rows : 3 * rows], sibling(theirs)
                own, residual = None, lax.ppermute(tie(incoming[0], done), "section", turn)
                continue
            if k + 1 < chips:
                blocks[k + 1] = tie(blocks[k + 1], summed)
                pre = up(k + 1)
                done = (pre, running)
                if k == 2:
                    residual = lax.ppermute(tie(incoming[0], pre), "section", turn)
            else:
                done = summed
            part = jnp.dot(act(k, done), down_weight[0], preferred_element_type=F32)
            theirs = part[rows:].astype(BF16)
            theirs = tie(theirs, (pres[k + 1][1], residual) if k + 1 < chips else (running, own))
            summed = part[:rows] + sibling(theirs).astype(F32) + running.astype(F32)
            summed = summed.astype(BF16)
            running = send(k, summed)
            if own is None:
                own = mine + tie(got, summed).astype(F32) + down_bias[0]
                own = lax.ppermute(own.astype(BF16), "section", turn)
        if own is None:
            own = lax.ppermute((mine + got.astype(F32) + down_bias[0]).astype(BF16), "section", turn)
        result = running.astype(F32) + own.astype(F32) + residual.astype(F32)
        return result.astype(BF16)[None]

    return per_device


def solution(mesh):
    placed = (
        P("section", "tensor", "dp"),
        P("section", "dp"),
        P("section", "dp"),
        P("section", "dp", "tensor"),
        P("section", "tensor"),
        P("section", "tensor", "dp"),
        P("section", "dp"),
    )

    def run(*args):
        body = make_per_device(
            args[0].shape[2], mesh.shape["section"], mesh.shape["dp"], mesh.shape["tensor"]
        )
        return jax.shard_map(
            body,
            mesh=mesh,
            in_specs=placed,
            out_specs=P("section", "tensor", "dp"),
            check_vma=False,
        )(*args)

    return run
```

```python
import jax
import jax.numpy as jnp
from jax import lax
from jax.sharding import PartitionSpec as P

F32 = jnp.float32
BF16 = jnp.bfloat16


def ring_order(n):
    return list(range(0, n, 2)) + list(range(1, n, 2))[::-1]


def make_per_device(width, n_section, n_dp, n_tensor):
    chips = n_tensor // 2
    order = ring_order(chips)
    along = [
        (order[i] * 2 + c, order[(i + 1) % chips] * 2 + c) for i in range(chips) for c in range(2)
    ]
    swap = [(i, i ^ 1) for i in range(n_tensor)]
    turn = [(i, (i + 1) % n_section) for i in range(n_section)]
    along_and_turn = [
        (s * n_tensor + a, t * n_tensor + b) for s, t in turn for a, b in along
    ]

    def forward(block):
        return lax.ppermute(block, "tensor", along)

    def sibling(block):
        return lax.ppermute(block, "tensor", swap)

    def from_others(sent):
        total = None
        for hop in range(1, n_dp):
            route = [(i, (i + hop) % n_dp) for i in range(n_dp)]
            got = lax.ppermute(sent, "dp", route)
            total = got if total is None else total.astype(F32) + got.astype(F32)
        return total

    def per_device(incoming, norm_gain, norm_shift, up_weight, up_bias, down_weight, down_bias):
        rows = incoming.shape[1]
        x = incoming[0].astype(F32)
        sums = jnp.stack(
            lax.reduce(
                (x, x * x), (F32(0), F32(0)), lambda a, b: (a[0] + b[0], a[1] + b[1]), (1,)
            )
        )
        total, square = sums + from_others(sums)
        mean = total / width
        var = square / width - mean * mean
        normed = (
            (x - mean[:, None]) * lax.rsqrt(var + 1e-05)[:, None] * norm_gain[0] + norm_shift[0]
        ).astype(BF16)

        blocks, pres = [(normed, sibling(normed))], []

        def tie(values, done):
            return lax.optimization_barrier((values, done))[0]

        def up(k):
            block = blocks[k][0]
            coming = forward(block) if k < chips - 1 else None
            both = jnp.concatenate(blocks[k], axis=0)
            pre = jnp.dot(both, up_weight[0], preferred_element_type=F32)
            other = from_others(pre.astype(BF16))
            if coming is not None:
                coming = tie(coming, (pre, pres[0][1]) if k == 1 else pre)
                blocks.append((coming, sibling(coming)))
            pres.append((pre, other))
            return pre

        def act(k, done):
            pre, other = pres[k]
            if done is not None:
                other = tie(other, done)
            return jax.nn.gelu(pre + other.astype(F32) + up_bias[0], approximate=True).astype(BF16)

        def send(k, value):
            if k < chips - 1:
                return forward(value)
            return lax.ppermute(value, ("section", "tensor"), along_and_turn)

        up(0)
        for k in range(1, chips):
            if k == 1:
                up(1)
                done = (pres[1][0], pres[0][1])
                if chips > 2:
                    blocks[2] = tie(blocks[2], done)
                    done = up(2)
                both = jnp.concatenate([act(1, done), act(0, None)], axis=0)
                part = jnp.dot(both, down_weight[0], preferred_element_type=F32)
                theirs = part[rows : 2 * rows].astype(BF16)
                if chips > 2:
                    theirs = tie(theirs, pres[2][1])
                summed = (part[:rows] + sibling(theirs).astype(F32)).astype(BF16)
                running = send(1, summed)
                theirs = tie(part[3 * rows :].astype(BF16), summed)
                own = part[2 * rows : 3 * rows] + sibling(theirs).astype(F32)
                own = lax.ppermute((own + down_bias[0] + x).astype(BF16), "section", turn)
                continue
            if k + 1 < chips:
                blocks[k + 1] = tie(blocks[k + 1], summed)
                done = (up(k + 1), running)
            else:
                done = summed
            part = jnp.dot(act(k, done), down_weight[0], preferred_element_type=F32)
            theirs = part[rows:].astype(BF16)
            theirs = tie(theirs, pres[k + 1][1] if k + 1 < chips else (running, own))
            summed = part[:rows] + sibling(theirs).astype(F32) + running.astype(F32)
            summed = summed.astype(BF16)
            running = send(k, summed)
        result = running.astype(F32) + own.astype(F32)
        return result.astype(BF16)[None]

    return per_device


def solution(mesh):
    placed = (
        P("section", "tensor", "dp"),
        P("section", "dp"),
        P("section", "dp"),
        P("section", "dp", "tensor"),
        P("section", "tensor"),
        P("section", "tensor", "dp"),
        P("section", "dp"),
    )

    def run(*args):
        body = make_per_device(
            args[0].shape[2], mesh.shape["section"], mesh.shape["dp"], mesh.shape["tensor"]
        )
        return jax.shard_map(
            body,
            mesh=mesh,
            in_specs=placed,
            out_specs=P("section", "tensor", "dp"),
            check_vma=False,
        )(*args)

    return run
```
